32 devices in a mesh: groups: 2 (over y), owners: 4 (over z), inner: 2 (over x), sub: 2 (over core).
Axes of the slice: x: 2, y: 2, z: 4, core: 2. Of those that a mesh axis runs over, the one named last changes fastest.
Arguments:
- embeddings: bfloat16 [16384, 4096], P(('groups', 'owners', 'inner'), 'sub'), parts along dimension 0, may hold values from -6 to 6
- pca_basis: bfloat16 [4096, 256], P('sub', 'inner'), may hold values from -0.09375 to 0.09375
- assignment: int32 [16384, 1], P(('groups', 'owners', 'inner', 'sub')), parts along dimension 0, may hold values from 0 to 31; in each aligned block of 512 rows (0 to 511, 512 to 1023, ...) at most 32 rows name the same one
- row_stamp: int32 [16384], P(('groups', 'owners', 'inner', 'sub')), parts along dimension 0, may hold values from 0 to 8191, each once
Outputs:
- similarity: float32 [16384], P(('groups', 'owners', 'inner', 'sub')), parts along dimension 0
- centroid: float32 [64, 256], P(('groups', 'owners', 'inner'), 'sub'), parts along dimension 0
The draws below stay inside these ranges and needn't reach their ends.
There are 2 independent parts, one for each index of `groups`. The reference program is written for one: setup_inputs(seed, part) draws one part's arguments, and reference() takes and returns one part's arrays. A program takes and returns all parts, laid end to end along the dimension named above; an argument that names none is the same for every part. Nothing has to cross between parts.
Inputs may be any that keep to these rules, and one draw needn't show every extreme that they name: `assignment`: among the 512 documents of one device no cluster is named more than 32 times; some cluster is named exactly 32 times by some device. `row_stamp`: A permutation of the documents.
All inputs are finite; a program needn't handle non-finite values.
Results may differ from the reference program's by a relative error of at most 0.0029.
Values may be sent and summed in bfloat16 or wider, within the bound.
A program may use at most 64 MiB of HBM per device.

```python
import math
import jax
import jax.numpy as jnp
import numpy as np
from jax import lax

E = 4096
P_SIZE = 256
ROW_DEV = 512
CLUSTERS = 32
MOST = 32
ROWS = 8192
N_OWNERS = 4
N_INNER = 2
N_SUB = 2


def block_scale(stream_key, shape, split, low, largest):
    def one(dim, blocks):
        steps = jax.random.uniform(jax.random.fold_in(jax.random.fold_in(stream_key, 6), dim), (blocks,), jnp.float32, low / len(split), largest / len(split))
        return jnp.repeat(jnp.exp(steps), shape[dim] // blocks).reshape((-1,) + (1,) * (len(shape) - dim - 1))

    level = one(*split[0])
    for cut in split[1:]:
        level = level * one(*cut)
    return level


def assign_block(own_key, own, number, rows, count, top, bound, skew):
    sequence = jax.random.permutation(own_key, count)
    packed, usual = shares(count, rows * top, bound, skew, True), shares(count, rows * top, bound, skew, False)
    places = jnp.arange(count)

    def named(tallies, rotation):
        used = int((tallies > 0).sum())
        fixed = max(1, used // 4)
        passed = fixed + (places - fixed + rotation * (used - fixed)) % max(1, count - fixed)
        return jnp.zeros((count,), jnp.int32).at[sequence[jnp.where(places < fixed, places, passed)]].set(jnp.asarray(tallies, jnp.int32))

    tallies = jnp.where(number % 4 == 0, named(packed, number // 4), named(usual, number - number // 4 - 1))
    mixed = jax.random.permutation(jax.random.fold_in(own, 3), count)
    donor, taker = mixed[0:count // 2 * 2:2], mixed[1:count // 2 * 2:2]
    margin = jnp.minimum(tallies[donor] - 1, bound - tallies[taker]) // 2
    margin = jnp.where((donor == sequence[0]) | (taker == sequence[0]) | (tallies[taker] == 0), 0, jnp.maximum(margin, 0))
    passed = jax.random.randint(jax.random.fold_in(own, 4), (count // 2,), 0, 1 << 20) % (margin + 1)
    tallies = tallies.at[donor].add(-passed).at[taker].add(passed)
    items = jnp.searchsorted(jnp.cumsum(tallies), jnp.arange(rows * top), side="right").astype(jnp.int32)
    grid = items.reshape(top, rows).T
    grid = grid[jax.random.permutation(jax.random.fold_in(own, 1), rows)]
    rotation = jax.random.randint(jax.random.fold_in(own, 2), (rows, 1), 0, top)
    return jnp.take_along_axis(grid, (jnp.arange(top)[None, :] + rotation) % top, axis=1)


def shares(amount, total, reach, lean, full):
    portions = [(1 << 20) // math.isqrt(rank ** lean) + 1 for rank in range(1, amount + 1)]
    largest = reach if full else min(reach, max(-(-total // amount), total * portions[0] // sum(portions)))
    least = 1 if total - largest >= amount - 1 else 0
    counts, spare = [largest] + [least] * (amount - 1), total - largest - least * (amount - 1)
    while spare > 0:
        movable = [i for i in range(1, amount) if counts[i] < largest] or [i for i in range(1, amount) if counts[i] < reach]
        whole, remaining = sum([portions[i] for i in movable]), spare
        for i in movable:
            extra = min(reach - counts[i], max(1, remaining * portions[i] // whole), spare)
            counts[i] = counts[i] + extra
            spare = spare - extra
    return np.array(counts)


def bell_draw(key, dims, spread, limit, shards=(), kind=jnp.bfloat16):
    factor_of = block_scale(key, dims, shards, -0.22, 0.18) if shards else 1.0
    result = jax.random.normal(key, dims, jnp.float32) * spread * factor_of
    return jnp.minimum(jnp.maximum(result, -limit), limit).astype(kind)


def setup_inputs(seed: int = 0, part: int = 0) -> dict:
    arg_keys = jax.random.split(jax.random.key(seed), 5)
    own_keys = jax.random.split(jax.random.fold_in(arg_keys[4], part), 5)
    embeddings = bell_draw(own_keys[0], (ROWS, E), 1.0, 6.0, ((0, 8), (1, 2)))
    pca_basis = bell_draw(arg_keys[1], (E, P_SIZE), E ** -0.5, 0.09375, ((0, 2), (1, 2)))
    assignment_keys = jax.random.split(jax.random.fold_in(own_keys[2], 1), ROWS // ROW_DEV)
    assignment_turns = jax.random.permutation(jax.random.fold_in(own_keys[2], 3), ROWS // ROW_DEV)
    assignment = jax.vmap(lambda own, number: assign_block(jax.random.fold_in(own_keys[2], 2), own, number, ROW_DEV, CLUSTERS, 1, MOST, 2))(assignment_keys, assignment_turns).reshape((ROWS, 1))
    row_stamp = jax.random.permutation(own_keys[3], ROWS).astype(jnp.int32)
    return dict(embeddings=embeddings, pca_basis=pca_basis, assignment=assignment, row_stamp=row_stamp)


EPS = 1e-06
SENTINEL = 1073741824

def reference(embeddings, pca_basis, assignment, row_stamp):
    projected = jnp.dot(embeddings, pca_basis, preferred_element_type=jnp.float32)
    unit = (projected * lax.rsqrt(lax.optimization_barrier(jnp.sum(projected * projected, axis=1, keepdims=True)) + EPS)).astype(jnp.bfloat16)
    labels = assignment[:, 0].astype(jnp.int32)
    row_total = labels.shape[0]
    ranked = jnp.argsort(labels, stable=True).astype(jnp.int32)
    sorted_labels = labels[ranked]
    totals = jnp.zeros((CLUSTERS,), jnp.int32).at[labels].add(1)
    starts = (jnp.cumsum(totals) - totals).astype(jnp.int32)
    within = jnp.arange(row_total, dtype=jnp.int32) - starts[sorted_labels]
    capacity = MOST * N_OWNERS * N_INNER * N_SUB
    table = jnp.full((CLUSTERS, capacity), row_total, jnp.int32).at[sorted_labels, within].set(ranked)
    padded_unit = jnp.concatenate([unit, jnp.zeros((1, unit.shape[1]), jnp.bfloat16)], axis=0)
    padded_stamp = jnp.concatenate([row_stamp.astype(jnp.int32), jnp.full((1,), SENTINEL, jnp.int32)])

    def one_cluster(members):
        vectors = padded_unit[members]
        stamps = padded_stamp[members]
        scores = jnp.dot(vectors, vectors.T, preferred_element_type=jnp.float32)
        earlier = stamps[None, :] < stamps[:, None]
        return lax.optimization_barrier(jnp.max(jnp.where(earlier, scores, jnp.float32(-1.0)), axis=1))
    highest = lax.map(one_cluster, table)
    similarity = jnp.zeros((row_total + 1,), jnp.float32).at[table.reshape(-1)].set(highest.reshape(-1))[:row_total]
    sums = jnp.zeros((CLUSTERS, unit.shape[1]), jnp.float32).at[labels].add(unit.astype(jnp.float32))
    centroid = sums * lax.rsqrt(lax.optimization_barrier(jnp.mean(sums * sums, axis=1, keepdims=True)) + EPS)
    return (similarity, centroid)
```

```python
import functools

import jax
import jax.numpy as jnp
from jax import lax
from jax.experimental import pallas as pl
from jax.experimental.pallas import tpu as pltpu
from jax.sharding import PartitionSpec as P

KDEV = 8


EPS = 1e-06
SENTINEL = 1073741824


def key_fold(queries, query_stamp, highest, piece):
    key_rows, key_stamp = piece
    groups = queries.shape[0]
    key_rows = jnp.swapaxes(key_rows, 0, 1).reshape(groups, -1, key_rows.shape[-1])
    key_stamp = jnp.swapaxes(key_stamp, 0, 1).reshape(groups, -1)
    scores = jnp.einsum("kqp,knp->kqn", queries, key_rows, preferred_element_type=jnp.float32)
    earlier = key_stamp[:, None, :] < query_stamp[:, :, None]
    return jnp.maximum(highest, jnp.max(jnp.where(earlier, scores, -1.0), axis=2))


def as_queries(incoming, incoming_stamp):
    groups = incoming.shape[1]
    queries = jnp.swapaxes(incoming, 0, 1).reshape(groups, -1, incoming.shape[-1])
    query_stamp = jnp.swapaxes(incoming_stamp, 0, 1).reshape(groups, -1)
    return (queries, query_stamp)


def per_device(embeddings, pca_basis, assignment, row_stamp):
    full_basis = lax.all_gather(pca_basis, "inner", axis=1, tiled=True)
    row_count = assignment.shape[0]
    projected = lax.psum_scatter(
        jnp.dot(embeddings, full_basis, preferred_element_type=jnp.float32),
        "sub",
        scatter_dimension=0,
        tiled=True,
    )
    unit = (
        projected * lax.rsqrt(jnp.sum(projected * projected, axis=1, keepdims=True) + EPS)
    ).astype(jnp.bfloat16)
    features = unit.shape[1]
    owners_n = lax.axis_size("owners")
    inner_n = lax.axis_size("inner")
    sub_n = lax.axis_size("sub")
    clusters = KDEV * owners_n
    slot_count = max(2, 2 * row_count // clusters)
    local_count = KDEV // inner_n
    labels = assignment[:, 0]
    one_hot = (labels[:, None] == jnp.arange(clusters, dtype=jnp.int32)[None, :]).astype(jnp.int32)
    before = jnp.cumsum(one_hot, axis=0) - one_hot
    rank = jnp.sum(before * one_hot, axis=1)
    position = labels * slot_count + rank
    source = (
        jnp.full((clusters * slot_count,), row_count, jnp.int32)
        .at[position]
        .set(jnp.arange(row_count, dtype=jnp.int32))
    )
    padded_unit = jnp.concatenate([unit, jnp.zeros((1, features), jnp.bfloat16)], axis=0)
    padded_stamp = jnp.concatenate([row_stamp, jnp.full((1,), SENTINEL, jnp.int32)])
    outgoing = padded_unit[source]
    outgoing_stamp = padded_stamp[source]
    incoming, incoming_stamp = (
        lax.all_to_all(
            outgoing.reshape(owners_n, KDEV * slot_count, features),
            "owners",
            split_axis=0,
            concat_axis=0,
            tiled=True,
        ),
        lax.all_to_all(
            outgoing_stamp.reshape(owners_n, KDEV * slot_count),
            "owners",
            split_axis=0,
            concat_axis=0,
            tiled=True,
        ),
    )
    incoming = incoming.reshape(owners_n, KDEV, slot_count, features)
    incoming_stamp = incoming_stamp.reshape(owners_n, KDEV, slot_count)
    queries, query_stamp = as_queries(incoming, incoming_stamp)
    start_best = jnp.full(query_stamp.shape, -1.0, jnp.float32)
    highest = key_fold(
        queries,
        query_stamp,
        start_best,
        (
            lax.all_gather(incoming, ("inner", "sub"), axis=0, tiled=True),
            lax.all_gather(incoming_stamp, ("inner", "sub"), axis=0, tiled=True),
        ),
    )
    answer = jnp.swapaxes(highest.reshape(KDEV, owners_n, slot_count), 0, 1).reshape(
        owners_n, KDEV * slot_count
    )
    returned = lax.all_to_all(answer, "owners", split_axis=0, concat_axis=0, tiled=True)
    partial_value = jnp.sum(incoming, axis=(0, 2), dtype=jnp.float32)
    half = features // sub_n
    arranged = jnp.transpose(
        partial_value.reshape(inner_n, local_count, sub_n, half), (0, 2, 1, 3)
    ).reshape(inner_n * sub_n * local_count, half)
    own_sums = lax.psum_scatter(arranged, ("inner", "sub"), scatter_dimension=0, tiled=True)
    similarity = returned.reshape(-1)[position]
    squares = lax.psum(jnp.sum(own_sums * own_sums, axis=1), "sub")
    centroid = own_sums * lax.rsqrt(squares[:, None] / features + EPS)
    return (similarity, centroid)


MESH = pl.DeviceIdType.MESH
CHUNKS = 4
BF = jnp.bfloat16
F32 = jnp.float32


def nt(a, b):
    return lax.dot_general(a, b, (((1,), (1,)), ((), ())), preferred_element_type=F32)


def mm(a, b):
    return jnp.dot(a, b, preferred_element_type=F32)


def row_to_column(row):
    return jnp.broadcast_to(row, (128, row.shape[1])).T[:, :1]


def fused_kernel(
    sizes, emb_hbm, basis_hbm, label_ref, stamp_ref, sim_ref, cent_ref,
    emb, own_basis, far_basis, place, half_out, half_in, outgoing, rows_in,
    meta_out, meta_in, ret_out, ret_in, cent_out, cent_in,
    emb_sem, basis_sem, x_send, x_recv, y_send, y_recv, sub_send, sub_recv,
    meta_send, meta_recv, row_send, row_recv, ret_send, ret_recv,
    cent_sem, local_sem,
):
    inner_n, sub_n, devices, slots = sizes
    row_count = label_ref.shape[1]
    g = lax.axis_index("groups")
    o = lax.axis_index("owners")
    i = lax.axis_index("inner")
    s = lax.axis_index("sub")
    chip = inner_n * sub_n
    me = o * chip + i * sub_n + s
    lane_base = (i * sub_n + s) * slots

    def coordinates(t):
        return (g, t // chip, (t // sub_n) % inner_n, t % sub_n)

    x_peer = (g, o, 1 - i, s)
    y_peer = (1 - g, o, i, s)
    sub_peer = (g, o, i, 1 - s)
    own_rows = pl.ds(pl.multiple_of(s * row_count, row_count), row_count)
    far_rows = pl.ds(pl.multiple_of((1 - s) * row_count, row_count), row_count)

    ret_in[...] = jnp.zeros_like(ret_in)
    load_far = pltpu.make_async_copy(emb_hbm.at[far_rows], emb.at[far_rows], emb_sem.at[0])
    load_own = pltpu.make_async_copy(emb_hbm.at[own_rows], emb.at[own_rows], emb_sem.at[1])
    load_basis = pltpu.make_async_copy(basis_hbm, own_basis, basis_sem)
    load_basis.start()
    load_far.start()
    load_own.start()

    barrier = pltpu.get_barrier_semaphore()

    def greet(j, carry):
        pl.semaphore_signal(
            barrier, inc=1, device_id=coordinates((me + j) % devices), device_id_type=MESH
        )
        return carry

    lax.fori_loop(1, devices, greet, 0)
    pl.semaphore_signal(barrier, inc=1, device_id=y_peer, device_id_type=MESH)
    pl.semaphore_wait(barrier, devices)

    depth = basis_hbm.shape[0]
    piece = depth // 2 // CHUNKS

    def span(group, c):
        return pl.ds(pl.multiple_of(group * (depth // 2) + c * piece, piece), piece)

    def x_copy(c):
        return pltpu.make_async_remote_copy(
            basis_hbm.at[span(g, c)], far_basis.at[span(g, c)],
            x_send.at[c], x_recv.at[c], device_id=x_peer, device_id_type=MESH,
        )

    def y_copy(c):
        return pltpu.make_async_remote_copy(
            far_basis.at[span(g, c)], far_basis.at[span(g, c)],
            y_send.at[c], y_recv.at[c], device_id=y_peer, device_id_type=MESH,
        )

    def y_arrival(c):
        return pltpu.make_async_remote_copy(
            far_basis.at[span(g, c)], far_basis.at[span(1 - g, c)],
            y_send.at[c], y_recv.at[c], device_id=y_peer, device_id_type=MESH,
        )

    for c in range(CHUNKS):
        x_copy(c).start()

    labels = label_ref[...]
    padded = (labels // 2) * 8 + labels % 2
    up = lax.broadcasted_iota(jnp.int32, (128, row_count), 0)
    member = up == padded
    one_hot = jnp.where(member, 1.0, 0.0)
    member_bf = one_hot.astype(BF)
    earlier_row = lax.broadcasted_iota(jnp.int32, (row_count, row_count), 0) < (
        lax.broadcasted_iota(jnp.int32, (row_count, row_count), 1)
    )
    before = mm(member_bf, jnp.where(earlier_row, 1.0, 0.0).astype(BF))
    rank = jnp.sum(before * one_hot, axis=0, keepdims=True).astype(jnp.int32)
    at_lane = up == rank + lane_base
    lane_hot = jnp.where(at_lane, 1.0, 0.0).astype(BF)
    coded = stamp_ref[...] + 1
    meta = jnp.zeros((128, 128), F32)
    for shift in (16, 8, 0):
        digit = ((coded >> shift) & 255).astype(F32)
        meta = meta + nt((one_hot * digit).astype(BF), lane_hot) * float(1 << shift)
    meta_out[...] = meta.reshape(devices, 8, 128)
    meta_in[me] = meta_out[me]

    def meta_copy(j):
        to = (me + j) % devices
        return pltpu.make_async_remote_copy(
            meta_out.at[to, pl.ds(0, 2)], meta_in.at[me, pl.ds(0, 2)],
            meta_send.at[j], meta_recv.at[j], device_id=coordinates(to), device_id_type=MESH,
        )

    def start_meta(j, carry):
        meta_copy(j).start()
        return carry

    lax.fori_loop(1, devices, start_meta, 0)
    position = labels * slots + rank
    place[...] = jnp.where(
        lax.broadcasted_iota(jnp.int32, (place.shape[0], row_count), 0) == position, 1.0, 0.0
    ).astype(BF)

    def half_copy(h):
        return pltpu.make_async_remote_copy(
            half_out.at[h], half_in.at[h], sub_send.at[h], sub_recv.at[h],
            device_id=sub_peer, device_id_type=MESH,
        )

    def column(h):
        return pl.ds(pl.multiple_of((i if h == 0 else 1 - i) * 128, 128), 128)

    my_slots = pl.ds(pl.multiple_of(me * slots, slots), slots)

    def row_copy(h, j):
        to = (me + j) % devices
        return pltpu.make_async_remote_copy(
            outgoing.at[h, pl.ds(to * 2, 2)], rows_in.at[:, my_slots, column(h)],
            row_send.at[h, j], row_recv.at[h, j],
            device_id=coordinates(to), device_id_type=MESH,
        )

    def own_copy(h):
        return pltpu.make_async_copy(
            outgoing.at[h, pl.ds(me * 2, 2)], rows_in.at[:, my_slots, column(h)], local_sem.at[h]
        )

    def send_half(h, own):
        half_copy(h).wait_recv()
        total = (own + half_in[h]).astype(BF)
        outgoing[h] = mm(place[...], total).astype(BF).reshape(outgoing.shape[1:])

        def start_rows(j, carry):
            row_copy(h, j).start()
            return carry

        lax.fori_loop(1, devices, start_rows, 0)
        own_copy(h).start()

    load_basis.wait()
    load_far.wait()
    half_out[0] = mm(emb[far_rows, :], own_basis[...])
    half_copy(0).start()
    load_own.wait()
    own = mm(emb[own_rows, :], own_basis[...])
    for c in range(2):
        x_copy(c).wait_recv()
        y_copy(c).start()
    send_half(0, own)
    for c in range(2, CHUNKS):
        x_copy(c).wait_recv()
        y_copy(c).start()

    for c in range(CHUNKS):
        y_arrival(c).wait_recv()
    half_out[1] = mm(emb[far_rows, :], far_basis[...])
    half_copy(1).start()
    own = mm(emb[own_rows, :], far_basis[...])
    send_half(1, own)

    for_meta = []

    def wait_meta(j, carry):
        meta_copy(j).wait_recv()
        return carry

    lax.fori_loop(1, devices, wait_meta, 0)
    for k in range(2):
        blocks = []
        for b in range(devices // chip):
            block = meta_in[b * chip, k:k + 1, :]
            for q in range(1, chip):
                block = block + meta_in[b * chip + q, k:k + 1, :]
            blocks.append(block)
        stamps = jnp.concatenate(blocks, axis=1)
        stamps = jnp.where(stamps == 0.0, float(SENTINEL), stamps)
        for_meta.append((stamps, row_to_column(stamps)))

    def wait_rows(j, carry):
        row_copy(0, j).wait_recv()
        row_copy(1, j).wait_recv()
        return carry

    lax.fori_loop(1, devices, wait_rows, 0)
    own_copy(0).wait()
    own_copy(1).wait()

    eye = lax.broadcasted_iota(jnp.int32, (128, 128), 0) == (
        lax.broadcasted_iota(jnp.int32, (128, 128), 1)
    )
    ret_out[...] = jnp.zeros_like(ret_out)
    inverses = []
    for k in range(2):
        keys = rows_in[k]
        scores = nt(keys, keys)
        blocks = [
            jnp.sum(
                jnp.where(eye, scores[b * 128:(b + 1) * 128, b * 128:(b + 1) * 128], 0.0),
                axis=0, keepdims=True,
            )
            for b in range(scores.shape[0] // 128)
        ]
        inverse = lax.rsqrt(jnp.concatenate(blocks, axis=1) + EPS)
        inverses.append(inverse)
        stamps, stamp_column = for_meta[k]
        scaled = scores * row_to_column(inverse)
        best = jnp.max(jnp.where(stamp_column < stamps, scaled, -jnp.inf), axis=0, keepdims=True)
        best = jnp.maximum(best * inverse, -1.0)
        for b in range(devices // chip):
            ret_out[b, k:k + 1, :] = best[:, b * 128:(b + 1) * 128]

    def ret_copy(j):
        to = (me + j) % devices
        return pltpu.make_async_remote_copy(
            ret_out.at[to // chip, pl.ds(0, 2)], ret_in.at[me, pl.ds(0, 2)],
            ret_send.at[j], ret_recv.at[j], device_id=coordinates(to), device_id_type=MESH,
        )

    def start_ret(j, carry):
        ret_copy(j).start()
        return carry

    lax.fori_loop(1, devices, start_ret, 0)
    ret_in[me] = ret_out[o]

    wide = rows_in.shape[2]
    cents = []
    for k in range(2):
        high = inverses[k].astype(BF)
        low = (inverses[k] - high.astype(F32)).astype(BF)
        keys = rows_in[k]
        fill = (8, inverses[k].shape[1])
        sums = (
            mm(jnp.broadcast_to(high, fill), keys) + mm(jnp.broadcast_to(low, fill), keys)
        )[:1]
        mean = jnp.sum(sums * sums, axis=1, keepdims=True) / wide
        cents.append(sums * lax.rsqrt(mean + EPS))
    cent_out[...] = jnp.zeros_like(cent_out)
    for k in range(2):
        left, right = cents[k][:, :128], cents[k][:, 128:]
        cent_out[k:k + 1, :] = jnp.where(s == 0, right, left)
    cent_copy = pltpu.make_async_remote_copy(
        cent_out, cent_in, cent_sem.at[0], cent_sem.at[1],
        device_id=sub_peer, device_id_type=MESH,
    )
    cent_copy.start()
    cent_copy.wait_recv()
    for k in range(2):
        mine = jnp.where(s == 0, cents[k][:, :128], cents[k][:, 128:])
        theirs = cent_in[k:k + 1, :]
        cent_ref[k:k + 1, :] = jnp.where(s == 0, mine, theirs)
        cent_ref[2 + k:3 + k, :] = jnp.where(s == 0, theirs, mine)

    def wait_ret(j, carry):
        ret_copy(j).wait_recv()
        return carry

    lax.fori_loop(1, devices, wait_ret, 0)
    answers = ret_in[...].reshape(128, 128).T
    picked = jnp.zeros((128, row_count), F32)
    for _ in range(3):
        part = answers.astype(BF)
        picked = picked + mm(part, member_bf)
        answers = answers - part.astype(F32)
    sim_ref[...] = jnp.sum(jnp.where(at_lane, picked, 0.0), axis=0, keepdims=True)

    def drain(j, carry):
        meta_copy(j).wait_send()
        row_copy(0, j).wait_send()
        row_copy(1, j).wait_send()
        ret_copy(j).wait_send()
        return carry

    lax.fori_loop(1, devices, drain, 0)
    for c in range(CHUNKS):
        x_copy(c).wait_send()
        y_copy(c).wait_send()
    for h in range(2):
        half_copy(h).wait_send()
    cent_copy.wait_send()


def fused(embeddings, pca_basis, assignment, row_stamp):
    row_count = assignment.shape[0]
    owners_n = lax.axis_size("owners")
    inner_n = lax.axis_size("inner")
    sub_n = lax.axis_size("sub")
    devices = owners_n * inner_n * sub_n
    clusters = KDEV * owners_n
    slots = 2 * row_count // clusters
    depth, part = pca_basis.shape
    wide = part * inner_n
    dma = pltpu.SemaphoreType.DMA
    hbm = pl.BlockSpec(memory_space=pl.ANY)
    vmem = pl.BlockSpec(memory_space=pltpu.VMEM)
    similarity, centroid = pl.pallas_call(
        functools.partial(fused_kernel, (inner_n, sub_n, devices, slots)),
        out_shape=(
            jax.ShapeDtypeStruct((1, row_count), F32),
            jax.ShapeDtypeStruct((KDEV // inner_n, wide // sub_n), F32),
        ),
        in_specs=[hbm, hbm, vmem, vmem],
        out_specs=(vmem, vmem),
        scratch_shapes=[
            pltpu.VMEM(embeddings.shape, BF),
            pltpu.VMEM((depth, part), BF),
            pltpu.VMEM((depth, part), BF),
            pltpu.VMEM((clusters * slots, row_count), BF),
            pltpu.VMEM((2, row_count, part), F32),
            pltpu.VMEM((2, row_count, part), F32),
            pltpu.VMEM((2, clusters, slots, part), BF),
            pltpu.VMEM((2, devices * slots, wide), BF),
            pltpu.VMEM((devices, 8, 128), F32),
            pltpu.VMEM((devices, 8, 128), F32),
            pltpu.VMEM((owners_n, 8, 128), F32),
            pltpu.VMEM((devices, 8, 128), F32),
            pltpu.VMEM((8, 128), F32),
            pltpu.VMEM((8, 128), F32),
            dma((2,)), dma, dma((CHUNKS,)), dma((CHUNKS,)), dma((CHUNKS,)), dma((CHUNKS,)),
            dma((2,)), dma((2,)),
            dma((devices,)), dma((devices,)),
            dma((2, devices)), dma((2, devices)),
            dma((devices,)), dma((devices,)),
            dma((2,)), dma((2,)),
        ],
        compiler_params=pltpu.CompilerParams(
            collective_id=0, has_side_effects=True, vmem_limit_bytes=48 * 1024 * 1024
        ),
        cost_estimate=pl.CostEstimate(
            flops=2 * embeddings.size * wide, bytes_accessed=2 * embeddings.size, transcendentals=0
        ),
    )(embeddings, pca_basis, assignment.reshape(1, row_count), row_stamp.reshape(1, row_count))
    return similarity.reshape(row_count), centroid


def fits(mesh):
    size = mesh.shape
    return (size["groups"], size["inner"], size["sub"], size["owners"]) == (2, 2, 2, 4)


def solution(mesh):
    in_specs = (
        P(("groups", "owners", "inner"), "sub"),
        P("sub", "inner"),
        P(("groups", "owners", "inner", "sub"), None),
        P(("groups", "owners", "inner", "sub")),
    )
    out_specs = (P(("groups", "owners", "inner", "sub")), P(("groups", "owners", "inner"), "sub"))
    return jax.shard_map(
        fused if fits(mesh) else per_device, mesh=mesh, in_specs=in_specs, out_specs=out_specs, check_vma=False
    )
```

```python
import functools

import jax
import jax.numpy as jnp
from jax import lax
from jax.experimental import pallas as pl
from jax.experimental.pallas import tpu as pltpu
from jax.sharding import PartitionSpec as P

KDEV = 8


EPS = 1e-06
SENTINEL = 1073741824


def key_fold(queries, query_stamp, highest, piece):
    key_rows, key_stamp = piece
    groups = queries.shape[0]
    key_rows = jnp.swapaxes(key_rows, 0, 1).reshape(groups, -1, key_rows.shape[-1])
    key_stamp = jnp.swapaxes(key_stamp, 0, 1).reshape(groups, -1)
    scores = jnp.einsum("kqp,knp->kqn", queries, key_rows, preferred_element_type=jnp.float32)
    earlier = key_stamp[:, None, :] < query_stamp[:, :, None]
    return jnp.maximum(highest, jnp.max(jnp.where(earlier, scores, -1.0), axis=2))


def as_queries(incoming, incoming_stamp):
    groups = incoming.shape[1]
    queries = jnp.swapaxes(incoming, 0, 1).reshape(groups, -1, incoming.shape[-1])
    query_stamp = jnp.swapaxes(incoming_stamp, 0, 1).reshape(groups, -1)
    return (queries, query_stamp)


def per_device(embeddings, pca_basis, assignment, row_stamp):
    full_basis = lax.all_gather(pca_basis, "inner", axis=1, tiled=True)
    row_count = assignment.shape[0]
    projected = lax.psum_scatter(
        jnp.dot(embeddings, full_basis, preferred_element_type=jnp.float32),
        "sub",
        scatter_dimension=0,
        tiled=True,
    )
    unit = (
        projected * lax.rsqrt(jnp.sum(projected * projected, axis=1, keepdims=True) + EPS)
    ).astype(jnp.bfloat16)
    features = unit.shape[1]
    owners_n = lax.axis_size("owners")
    inner_n = lax.axis_size("inner")
    sub_n = lax.axis_size("sub")
    clusters = KDEV * owners_n
    slot_count = max(2, 2 * row_count // clusters)
    local_count = KDEV // inner_n
    labels = assignment[:, 0]
    one_hot = (labels[:, None] == jnp.arange(clusters, dtype=jnp.int32)[None, :]).astype(jnp.int32)
    before = jnp.cumsum(one_hot, axis=0) - one_hot
    rank = jnp.sum(before * one_hot, axis=1)
    position = labels * slot_count + rank
    source = (
        jnp.full((clusters * slot_count,), row_count, jnp.int32)
        .at[position]
        .set(jnp.arange(row_count, dtype=jnp.int32))
    )
    padded_unit = jnp.concatenate([unit, jnp.zeros((1, features), jnp.bfloat16)], axis=0)
    padded_stamp = jnp.concatenate([row_stamp, jnp.full((1,), SENTINEL, jnp.int32)])
    outgoing = padded_unit[source]
    outgoing_stamp = padded_stamp[source]
    incoming, incoming_stamp = (
        lax.all_to_all(
            outgoing.reshape(owners_n, KDEV * slot_count, features),
            "owners",
            split_axis=0,
            concat_axis=0,
            tiled=True,
        ),
        lax.all_to_all(
            outgoing_stamp.reshape(owners_n, KDEV * slot_count),
            "owners",
            split_axis=0,
            concat_axis=0,
            tiled=True,
        ),
    )
    incoming = incoming.reshape(owners_n, KDEV, slot_count, features)
    incoming_stamp = incoming_stamp.reshape(owners_n, KDEV, slot_count)
    queries, query_stamp = as_queries(incoming, incoming_stamp)
    start_best = jnp.full(query_stamp.shape, -1.0, jnp.float32)
    highest = key_fold(
        queries,
        query_stamp,
        start_best,
        (
            lax.all_gather(incoming, ("inner", "sub"), axis=0, tiled=True),
            lax.all_gather(incoming_stamp, ("inner", "sub"), axis=0, tiled=True),
        ),
    )
    answer = jnp.swapaxes(highest.reshape(KDEV, owners_n, slot_count), 0, 1).reshape(
        owners_n, KDEV * slot_count
    )
    returned = lax.all_to_all(answer, "owners", split_axis=0, concat_axis=0, tiled=True)
    partial_value = jnp.sum(incoming, axis=(0, 2), dtype=jnp.float32)
    half = features // sub_n
    arranged = jnp.transpose(
        partial_value.reshape(inner_n, local_count, sub_n, half), (0, 2, 1, 3)
    ).reshape(inner_n * sub_n * local_count, half)
    own_sums = lax.psum_scatter(arranged, ("inner", "sub"), scatter_dimension=0, tiled=True)
    similarity = returned.reshape(-1)[position]
    squares = lax.psum(jnp.sum(own_sums * own_sums, axis=1), "sub")
    centroid = own_sums * lax.rsqrt(squares[:, None] / features + EPS)
    return (similarity, centroid)


MESH = pl.DeviceIdType.MESH
CHUNKS = 4
BF = jnp.bfloat16
F32 = jnp.float32


def nt(a, b):
    return lax.dot_general(a, b, (((1,), (1,)), ((), ())), preferred_element_type=F32)


def mm(a, b):
    return jnp.dot(a, b, preferred_element_type=F32)


def row_to_column(row):
    return jnp.broadcast_to(row, (128, row.shape[1])).T[:, :1]


def fused_kernel(
    sizes, emb_hbm, basis_hbm, label_hbm, stamp_hbm, sim_ref, cent_ref,
    emb, own_basis, far_basis, place, half_out, half_in, outgoing, rows_in,
    meta_out, meta_in, ret_out, ret_in, cent_out, cent_in,
    emb_sem, basis_sem, x_send, x_recv, y_send, y_recv, sub_send, sub_recv,
    meta_send, meta_recv, row_send, row_recv, ret_send, ret_recv,
    cent_sem, local_sem, label_ref, stamp_ref,
):
    inner_n, sub_n, devices, slots = sizes
    row_count = label_hbm.shape[1]
    g = lax.axis_index("groups")
    o = lax.axis_index("owners")
    i = lax.axis_index("inner")
    s = lax.axis_index("sub")
    chip = inner_n * sub_n
    me = o * chip + i * sub_n + s
    lane_base = (i * sub_n + s) * slots

    owners_n = devices // chip
    peers = []
    for step in (2, 3, 1, 0):
        owner = (o + step) % owners_n
        for inner in (1 - i, i):
            for sub in (1 - s, s):
                if step or inner is not i or sub is not s:
                    number = owner * chip + inner * sub_n + sub
                    peers.append(((g, owner, inner, sub), owner, number))

    x_peer = (g, o, 1 - i, s)
    y_peer = (1 - g, o, i, s)
    sub_peer = (g, o, i, 1 - s)
    own_rows = pl.ds(pl.multiple_of(s * row_count, row_count), row_count)
    far_rows = pl.ds(pl.multiple_of((1 - s) * row_count, row_count), row_count)

    load_far = pltpu.make_async_copy(emb_hbm.at[far_rows], emb.at[far_rows], emb_sem.at[0])
    load_own = pltpu.make_async_copy(emb_hbm.at[own_rows], emb.at[own_rows], emb_sem.at[1])
    load_basis = pltpu.make_async_copy(basis_hbm, own_basis, basis_sem)
    load_labels = pltpu.make_async_copy(label_hbm, label_ref, local_sem.at[2])
    load_stamps = pltpu.make_async_copy(stamp_hbm, stamp_ref, local_sem.at[3])
    load_labels.start()
    load_stamps.start()
    load_basis.start()
    load_far.start()
    load_own.start()

    barrier = pltpu.get_barrier_semaphore()

    ret_in[...] = jnp.zeros_like(ret_in)
    for target in [peer[0] for peer in peers] + [y_peer]:
        pl.semaphore_signal(barrier, inc=1, device_id=target, device_id_type=MESH)

    depth = basis_hbm.shape[0]
    piece = depth // 2 // CHUNKS

    def span(group, c):
        return pl.ds(pl.multiple_of(group * (depth // 2) + c * piece, piece), piece)

    def x_copy(c):
        return pltpu.make_async_remote_copy(
            basis_hbm.at[span(g, c)], far_basis.at[span(g, c)],
            x_send.at[c], x_recv.at[c], device_id=x_peer, device_id_type=MESH,
        )

    def y_copy(c):
        return pltpu.make_async_remote_copy(
            far_basis.at[span(g, c)], far_basis.at[span(g, c)],
            y_send.at[c], y_recv.at[c], device_id=y_peer, device_id_type=MESH,
        )

    def y_arrival(c):
        return pltpu.make_async_remote_copy(
            far_basis.at[span(g, c)], far_basis.at[span(1 - g, c)],
            y_send.at[c], y_recv.at[c], device_id=y_peer, device_id_type=MESH,
        )

    load_labels.wait()
    load_stamps.wait()
    labels = label_ref[...]
    padded = (labels // 2) * 8 + labels % 2
    up = lax.broadcasted_iota(jnp.int32, (128, row_count), 0)
    member = up == padded
    one_hot = jnp.where(member, 1.0, 0.0)
    member_bf = one_hot.astype(BF)
    earlier_row = lax.broadcasted_iota(jnp.int32, (row_count, row_count), 0) < (
        lax.broadcasted_iota(jnp.int32, (row_count, row_count), 1)
    )
    before = mm(member_bf, jnp.where(earlier_row, 1.0, 0.0).astype(BF))
    rank = jnp.sum(before * one_hot, axis=0, keepdims=True).astype(jnp.int32)
    at_lane = up == rank + lane_base
    lane_hot = jnp.where(at_lane, 1.0, 0.0).astype(BF)
    coded = stamp_ref[...] + 1
    meta = jnp.zeros((128, 128), F32)
    for shift in (16, 8, 0):
        digit = ((coded >> shift) & 255).astype(F32)
        meta = meta + nt((one_hot * digit).astype(BF), lane_hot) * float(1 << shift)
    meta_out[...] = meta.reshape(devices, 8, 128)
    meta_in[me] = meta_out[me]

    pl.semaphore_wait(barrier, devices)
    for c in range(CHUNKS):
        x_copy(c).start()
    for target, owner, number in peers:
        pltpu.make_async_remote_copy(
            meta_out.at[number, pl.ds(0, 2)], meta_in.at[me, pl.ds(0, 2)],
            meta_send, meta_recv, device_id=target, device_id_type=MESH,
        ).start()
    position = labels * slots + rank
    place[...] = jnp.where(
        lax.broadcasted_iota(jnp.int32, (place.shape[0], row_count), 0) == position, 1.0, 0.0
    ).astype(BF)

    def half_copy(h):
        return pltpu.make_async_remote_copy(
            half_out.at[h], half_in.at[h], sub_send.at[h], sub_recv.at[h],
            device_id=sub_peer, device_id_type=MESH,
        )

    def column(h):
        return pl.ds(pl.multiple_of((i if h == 0 else 1 - i) * 128, 128), 128)

    my_slots = pl.ds(pl.multiple_of(me * slots, slots), slots)

    def all_rows(sem):
        part = outgoing.at[0, pl.ds(0, 2 * (devices - 1))]
        return pltpu.make_async_copy(part, part, sem)

    def all_small(sem):
        part = meta_out.at[pl.ds(0, devices - 1), pl.ds(0, 2)]
        return pltpu.make_async_copy(part, part, sem)

    def own_copy(h):
        return pltpu.make_async_copy(
            outgoing.at[h, pl.ds(me * 2, 2)], rows_in.at[:, my_slots, column(h)], local_sem.at[h]
        )

    def send_half(h, own):
        half_copy(h).wait_recv()
        total = (own + half_in[h]).astype(BF)
        outgoing[h] = mm(place[...], total).astype(BF).reshape(outgoing.shape[1:])

        for target, owner, number in peers:
            pltpu.make_async_remote_copy(
                outgoing.at[h, pl.ds(number * 2, 2)], rows_in.at[:, my_slots, column(h)],
                row_send.at[h], row_recv.at[h], device_id=target, device_id_type=MESH,
            ).start()
        own_copy(h).start()

    load_basis.wait()
    load_far.wait()
    half_out[0] = mm(emb[far_rows, :], own_basis[...])
    half_copy(0).start()
    load_own.wait()
    own = mm(emb[own_rows, :], own_basis[...])
    for c in range(2):
        x_copy(c).wait_recv()
        y_copy(c).start()
    send_half(0, own)
    for c in range(2, CHUNKS):
        x_copy(c).wait_recv()
        y_copy(c).start()

    for c in range(CHUNKS):
        y_arrival(c).wait_recv()
    half_out[1] = mm(emb[far_rows, :], far_basis[...])
    half_copy(1).start()
    own = mm(emb[own_rows, :], far_basis[...])
    send_half(1, own)

    for_meta = []

    all_small(meta_recv).wait()
    for k in range(2):
        blocks = []
        for b in range(devices // chip):
            block = meta_in[b * chip, k:k + 1, :]
            for q in range(1, chip):
                block = block + meta_in[b * chip + q, k:k + 1, :]
            blocks.append(block)
        stamps = jnp.concatenate(blocks, axis=1)
        stamps = jnp.where(stamps == 0.0, float(SENTINEL), stamps)
        for_meta.append((stamps, row_to_column(stamps)))

    all_rows(row_recv.at[0]).wait()
    all_rows(row_recv.at[1]).wait()
    own_copy(0).wait()
    own_copy(1).wait()

    eye = lax.broadcasted_iota(jnp.int32, (128, 128), 0) == (
        lax.broadcasted_iota(jnp.int32, (128, 128), 1)
    )
    ret_out[...] = jnp.zeros_like(ret_out)
    inverses = []
    for k in range(2):
        keys = rows_in[k]
        scores = nt(keys, keys)
        blocks = [
            jnp.sum(
                jnp.where(eye, scores[b * 128:(b + 1) * 128, b * 128:(b + 1) * 128], 0.0),
                axis=0, keepdims=True,
            )
            for b in range(scores.shape[0] // 128)
        ]
        inverse = lax.rsqrt(jnp.concatenate(blocks, axis=1) + EPS)
        inverses.append(inverse)
        stamps, stamp_column = for_meta[k]
        scaled = scores * row_to_column(inverse)
        best = jnp.max(jnp.where(stamp_column < stamps, scaled, -jnp.inf), axis=0, keepdims=True)
        best = jnp.maximum(best * inverse, -1.0)
        for b in range(devices // chip):
            ret_out[b, k:k + 1, :] = best[:, b * 128:(b + 1) * 128]

    for target, owner, number in peers:
        pltpu.make_async_remote_copy(
            ret_out.at[owner, pl.ds(0, 2)], ret_in.at[me, pl.ds(0, 2)],
            ret_send, ret_recv, device_id=target, device_id_type=MESH,
        ).start()
    ret_in[me] = ret_out[o]

    wide = rows_in.shape[2]
    cents = []
    for k in range(2):
        high = inverses[k].astype(BF)
        low = (inverses[k] - high.astype(F32)).astype(BF)
        keys = rows_in[k]
        fill = (8, inverses[k].shape[1])
        sums = (
            mm(jnp.broadcast_to(high, fill), keys) + mm(jnp.broadcast_to(low, fill), keys)
        )[:1]
        mean = jnp.sum(sums * sums, axis=1, keepdims=True) / wide
        cents.append(sums * lax.rsqrt(mean + EPS))
    cent_out[...] = jnp.zeros_like(cent_out)
    for k in range(2):
        left, right = cents[k][:, :128], cents[k][:, 128:]
        cent_out[k:k + 1, :] = jnp.where(s == 0, right, left)
    cent_copy = pltpu.make_async_remote_copy(
        cent_out, cent_in, cent_sem.at[0], cent_sem.at[1],
        device_id=sub_peer, device_id_type=MESH,
    )
    cent_copy.start()
    cent_copy.wait_recv()
    for k in range(2):
        mine = jnp.where(s == 0, cents[k][:, :128], cents[k][:, 128:])
        theirs = cent_in[k:k + 1, :]
        cent_ref[k:k + 1, :] = jnp.where(s == 0, mine, theirs)
        cent_ref[2 + k:3 + k, :] = jnp.where(s == 0, theirs, mine)

    all_small(ret_recv).wait()
    answers = ret_in[...].reshape(128, 128).T
    picked = jnp.zeros((128, row_count), F32)
    for _ in range(3):
        part = answers.astype(BF)
        picked = picked + mm(part, member_bf)
        answers = answers - part.astype(F32)
    sim_ref[...] = jnp.sum(jnp.where(at_lane, picked, 0.0), axis=0, keepdims=True)

    all_small(meta_send).wait()
    all_small(ret_send).wait()
    for h in range(2):
        all_rows(row_send.at[h]).wait()
    for c in range(CHUNKS):
        x_copy(c).wait_send()
        y_copy(c).wait_send()
    for h in range(2):
        half_copy(h).wait_send()
    cent_copy.wait_send()


def fused(embeddings, pca_basis, assignment, row_stamp):
    row_count = assignment.shape[0]
    owners_n = lax.axis_size("owners")
    inner_n = lax.axis_size("inner")
    sub_n = lax.axis_size("sub")
    devices = owners_n * inner_n * sub_n
    clusters = KDEV * owners_n
    slots = 2 * row_count // clusters
    depth, part = pca_basis.shape
    wide = part * inner_n
    dma = pltpu.SemaphoreType.DMA
    hbm = pl.BlockSpec(memory_space=pltpu.HBM)
    vmem = pl.BlockSpec(memory_space=pltpu.VMEM)
    similarity, centroid = pl.pallas_call(
        functools.partial(fused_kernel, (inner_n, sub_n, devices, slots)),
        out_shape=(
            jax.ShapeDtypeStruct((1, row_count), F32),
            jax.ShapeDtypeStruct((KDEV // inner_n, wide // sub_n), F32),
        ),
        in_specs=[hbm, hbm, hbm, hbm],
        out_specs=(vmem, vmem),
        scratch_shapes=[
            pltpu.VMEM(embeddings.shape, BF),
            pltpu.VMEM((depth, part), BF),
            pltpu.VMEM((depth, part), BF),
            pltpu.VMEM((clusters * slots, row_count), BF),
            pltpu.VMEM((2, row_count, part), F32),
            pltpu.VMEM((2, row_count, part), F32),
            pltpu.VMEM((2, clusters, slots, part), BF),
            pltpu.VMEM((2, devices * slots, wide), BF),
            pltpu.VMEM((devices, 8, 128), F32),
            pltpu.VMEM((devices, 8, 128), F32),
            pltpu.VMEM((owners_n, 8, 128), F32),
            pltpu.VMEM((devices, 8, 128), F32),
            pltpu.VMEM((8, 128), F32),
            pltpu.VMEM((8, 128), F32),
            dma((2,)), dma, dma((CHUNKS,)), dma((CHUNKS,)), dma((CHUNKS,)), dma((CHUNKS,)),
            dma((2,)), dma((2,)),
            dma, dma, dma((2,)), dma((2,)), dma, dma,
            dma((2,)), dma((4,)),
            pltpu.VMEM((1, row_count), jnp.int32),
            pltpu.VMEM((1, row_count), jnp.int32),
        ],
        compiler_params=pltpu.CompilerParams(
            collective_id=0, has_side_effects=True, vmem_limit_bytes=60 * 1024 * 1024
        ),
        cost_estimate=pl.CostEstimate(
            flops=2 * embeddings.size * wide, bytes_accessed=2 * embeddings.size, transcendentals=0
        ),
    )(embeddings, pca_basis, assignment.reshape(1, row_count), row_stamp.reshape(1, row_count))
    return similarity.reshape(row_count), centroid


def fits(mesh):
    size = mesh.shape
    return (size["groups"], size["inner"], size["sub"], size["owners"]) == (2, 2, 2, 4)


def solution(mesh):
    in_specs = (
        P(("groups", "owners", "inner"), "sub"),
        P("sub", "inner"),
        P(("groups", "owners", "inner", "sub"), None),
        P(("groups", "owners", "inner", "sub")),
    )
    out_specs = (P(("groups", "owners", "inner", "sub")), P(("groups", "owners", "inner"), "sub"))
    return jax.shard_map(
        fused if fits(mesh) else per_device, mesh=mesh, in_specs=in_specs, out_specs=out_specs, check_vma=False
    )
```

```python
import functools

import jax
import jax.numpy as jnp
from jax import lax
from jax.experimental import pallas as pl
from jax.experimental.pallas import tpu as pltpu
from jax.sharding import PartitionSpec as P

KDEV = 8


EPS = 1e-06
SENTINEL = 1073741824


def key_fold(queries, query_stamp, highest, piece):
    key_rows, key_stamp = piece
    groups = queries.shape[0]
    key_rows = jnp.swapaxes(key_rows, 0, 1).reshape(groups, -1, key_rows.shape[-1])
    key_stamp = jnp.swapaxes(key_stamp, 0, 1).reshape(groups, -1)
    scores = jnp.einsum("kqp,knp->kqn", queries, key_rows, preferred_element_type=jnp.float32)
    earlier = key_stamp[:, None, :] < query_stamp[:, :, None]
    return jnp.maximum(highest, jnp.max(jnp.where(earlier, scores, -1.0), axis=2))


def as_queries(incoming, incoming_stamp):
    groups = incoming.shape[1]
    queries = jnp.swapaxes(incoming, 0, 1).reshape(groups, -1, incoming.shape[-1])
    query_stamp = jnp.swapaxes(incoming_stamp, 0, 1).reshape(groups, -1)
    return (queries, query_stamp)


def per_device(embeddings, pca_basis, assignment, row_stamp):
    full_basis = lax.all_gather(pca_basis, "inner", axis=1, tiled=True)
    row_count = assignment.shape[0]
    projected = lax.psum_scatter(
        jnp.dot(embeddings, full_basis, preferred_element_type=jnp.float32),
        "sub",
        scatter_dimension=0,
        tiled=True,
    )
    unit = (
        projected * lax.rsqrt(jnp.sum(projected * projected, axis=1, keepdims=True) + EPS)
    ).astype(jnp.bfloat16)
    features = unit.shape[1]
    owners_n = lax.axis_size("owners")
    inner_n = lax.axis_size("inner")
    sub_n = lax.axis_size("sub")
    clusters = KDEV * owners_n
    slot_count = max(2, 2 * row_count // clusters)
    local_count = KDEV // inner_n
    labels = assignment[:, 0]
    one_hot = (labels[:, None] == jnp.arange(clusters, dtype=jnp.int32)[None, :]).astype(jnp.int32)
    before = jnp.cumsum(one_hot, axis=0) - one_hot
    rank = jnp.sum(before * one_hot, axis=1)
    position = labels * slot_count + rank
    source = (
        jnp.full((clusters * slot_count,), row_count, jnp.int32)
        .at[position]
        .set(jnp.arange(row_count, dtype=jnp.int32))
    )
    padded_unit = jnp.concatenate([unit, jnp.zeros((1, features), jnp.bfloat16)], axis=0)
    padded_stamp = jnp.concatenate([row_stamp, jnp.full((1,), SENTINEL, jnp.int32)])
    outgoing = padded_unit[source]
    outgoing_stamp = padded_stamp[source]
    incoming, incoming_stamp = (
        lax.all_to_all(
            outgoing.reshape(owners_n, KDEV * slot_count, features),
            "owners",
            split_axis=0,
            concat_axis=0,
            tiled=True,
        ),
        lax.all_to_all(
            outgoing_stamp.reshape(owners_n, KDEV * slot_count),
            "owners",
            split_axis=0,
            concat_axis=0,
            tiled=True,
        ),
    )
    incoming = incoming.reshape(owners_n, KDEV, slot_count, features)
    incoming_stamp = incoming_stamp.reshape(owners_n, KDEV, slot_count)
    queries, query_stamp = as_queries(incoming, incoming_stamp)
    start_best = jnp.full(query_stamp.shape, -1.0, jnp.float32)
    highest = key_fold(
        queries,
        query_stamp,
        start_best,
        (
            lax.all_gather(incoming, ("inner", "sub"), axis=0, tiled=True),
            lax.all_gather(incoming_stamp, ("inner", "sub"), axis=0, tiled=True),
        ),
    )
    answer = jnp.swapaxes(highest.reshape(KDEV, owners_n, slot_count), 0, 1).reshape(
        owners_n, KDEV * slot_count
    )
    returned = lax.all_to_all(answer, "owners", split_axis=0, concat_axis=0, tiled=True)
    partial_value = jnp.sum(incoming, axis=(0, 2), dtype=jnp.float32)
    half = features // sub_n
    arranged = jnp.transpose(
        partial_value.reshape(inner_n, local_count, sub_n, half), (0, 2, 1, 3)
    ).reshape(inner_n * sub_n * local_count, half)
    own_sums = lax.psum_scatter(arranged, ("inner", "sub"), scatter_dimension=0, tiled=True)
    similarity = returned.reshape(-1)[position]
    squares = lax.psum(jnp.sum(own_sums * own_sums, axis=1), "sub")
    centroid = own_sums * lax.rsqrt(squares[:, None] / features + EPS)
    return (similarity, centroid)


MESH = pl.DeviceIdType.MESH
CHUNKS = 4
BANDS = 2
BF = jnp.bfloat16
F32 = jnp.float32


def nt(a, b):
    return lax.dot_general(a, b, (((1,), (1,)), ((), ())), preferred_element_type=F32)


def mm(a, b):
    return jnp.dot(a, b, preferred_element_type=F32)


def row_to_column(row):
    return jnp.broadcast_to(row, (128, row.shape[1])).T[:, :1]


def fused_kernel(
    sizes, emb_hbm, basis_hbm, label_hbm, stamp_hbm, sim_ref, cent_ref,
    emb, own_basis, far_basis, place, half_out, half_in, outgoing, rows_in,
    meta_out, meta_in, ret_out, ret_in, cent_out, cent_in,
    emb_sem, basis_sem, x_send, x_recv, y_send, y_recv, sub_send, sub_recv,
    meta_send, meta_recv, row_send, row_recv, ret_send, ret_recv,
    cent_sem, local_sem, label_ref, stamp_ref, kept,
):
    inner_n, sub_n, devices, slots = sizes
    row_count = label_hbm.shape[1]
    g = lax.axis_index("groups")
    o = lax.axis_index("owners")
    i = lax.axis_index("inner")
    s = lax.axis_index("sub")
    chip = inner_n * sub_n
    me = o * chip + i * sub_n + s
    lane_base = (i * sub_n + s) * slots

    owners_n = devices // chip
    peers = []
    for step in (2, 3, 1, 0):
        owner = (o + step) % owners_n
        for inner in (1 - i, i):
            for sub in (1 - s, s):
                if step or inner is not i or sub is not s:
                    number = owner * chip + inner * sub_n + sub
                    peers.append(((g, owner, inner, sub), owner, number))

    x_peer = (g, o, 1 - i, s)
    y_peer = (1 - g, o, i, s)
    sub_peer = (g, o, i, 1 - s)
    own_rows = pl.ds(pl.multiple_of(s * row_count, row_count), row_count)
    far_rows = pl.ds(pl.multiple_of((1 - s) * row_count, row_count), row_count)

    depth = basis_hbm.shape[0]
    middle = depth // 2
    spans = [pl.ds(pl.multiple_of(part * middle, middle), middle) for part in (g, 1 - g)]
    load_far = [
        pltpu.make_async_copy(emb_hbm.at[far_rows, spans[p]], emb.at[p, far_rows], emb_sem.at[p])
        for p in range(2)
    ]
    load_own = [
        pltpu.make_async_copy(emb_hbm.at[own_rows, spans[p]], emb.at[p, own_rows], emb_sem.at[2 + p])
        for p in range(2)
    ]
    load_basis = [
        pltpu.make_async_copy(basis_hbm.at[spans[p]], own_basis.at[p], basis_sem.at[p])
        for p in range(2)
    ]
    load_labels = pltpu.make_async_copy(label_hbm, label_ref, local_sem.at[2])
    load_stamps = pltpu.make_async_copy(stamp_hbm, stamp_ref, local_sem.at[3])
    load_labels.start()
    load_stamps.start()
    for load in load_basis + load_far + load_own:
        load.start()

    barrier = pltpu.get_barrier_semaphore()

    ret_in[...] = jnp.zeros_like(ret_in)
    for target in [peer[0] for peer in peers] + [y_peer]:
        pl.semaphore_signal(barrier, inc=1, device_id=target, device_id_type=MESH)

    piece = middle // CHUNKS

    def x_copy(c):
        rows = pl.ds(pl.multiple_of(g * middle + c * piece, piece), piece)
        return pltpu.make_async_remote_copy(
            basis_hbm.at[rows], far_basis.at[0, pl.ds(c * piece, piece)],
            x_send.at[c], x_recv.at[c], device_id=x_peer, device_id_type=MESH,
        )

    def y_copy(c):
        rows = pl.ds(c * piece, piece)
        return pltpu.make_async_remote_copy(
            far_basis.at[0, rows], far_basis.at[1, rows],
            y_send.at[c], y_recv.at[c], device_id=y_peer, device_id_type=MESH,
        )

    load_labels.wait()
    load_stamps.wait()
    labels = label_ref[...]
    padded = (labels // 2) * 8 + labels % 2
    up = lax.broadcasted_iota(jnp.int32, (128, row_count), 0)
    member = up == padded
    one_hot = jnp.where(member, 1.0, 0.0)
    member_bf = one_hot.astype(BF)
    earlier_row = lax.broadcasted_iota(jnp.int32, (row_count, row_count), 0) < (
        lax.broadcasted_iota(jnp.int32, (row_count, row_count), 1)
    )
    before = mm(member_bf, jnp.where(earlier_row, 1.0, 0.0).astype(BF))
    rank = jnp.sum(before * one_hot, axis=0, keepdims=True).astype(jnp.int32)
    at_lane = up == rank + lane_base
    lane_hot = jnp.where(at_lane, 1.0, 0.0).astype(BF)
    coded = stamp_ref[...] + 1
    meta = jnp.zeros((128, 128), F32)
    for shift in (16, 8, 0):
        digit = ((coded >> shift) & 255).astype(F32)
        meta = meta + nt((one_hot * digit).astype(BF), lane_hot) * float(1 << shift)
    meta_out[...] = meta.reshape(devices, 8, 128)
    meta_in[me] = meta_out[me]

    pl.semaphore_wait(barrier, devices)
    for c in range(CHUNKS):
        x_copy(c).start()
    for target, owner, number in peers:
        pltpu.make_async_remote_copy(
            meta_out.at[number, pl.ds(0, 2)], meta_in.at[me, pl.ds(0, 2)],
            meta_send, meta_recv, device_id=target, device_id_type=MESH,
        ).start()
    position = labels * slots + rank
    place[...] = jnp.where(
        lax.broadcasted_iota(jnp.int32, (place.shape[0], row_count), 0) == position, 1.0, 0.0
    ).astype(BF)

    band = row_count // BANDS

    def half_copy(h, b):
        rows = pl.ds(b * band, band)
        return pltpu.make_async_remote_copy(
            half_out.at[h, rows], half_in.at[h, rows], sub_send.at[h, b], sub_recv.at[h, b],
            device_id=sub_peer, device_id_type=MESH,
        )

    def far_band(b):
        start = pl.multiple_of((1 - s) * row_count + b * band, band)
        return pl.ds(start, band)

    def column(h):
        return pl.ds(pl.multiple_of((i if h == 0 else 1 - i) * 128, 128), 128)

    my_slots = pl.ds(pl.multiple_of(me * slots, slots), slots)

    def all_rows(sem):
        part = outgoing.at[0, pl.ds(0, 2 * (devices - 1))]
        return pltpu.make_async_copy(part, part, sem)

    def all_small(sem):
        part = meta_out.at[pl.ds(0, devices - 1), pl.ds(0, 2)]
        return pltpu.make_async_copy(part, part, sem)

    def own_copy(h):
        return pltpu.make_async_copy(
            outgoing.at[h, pl.ds(me * 2, 2)], rows_in.at[:, my_slots, column(h)], local_sem.at[h]
        )

    def send_half(h, own):
        for b in range(BANDS):
            half_copy(h, b).wait_recv()
        total = (own + half_in[h]).astype(BF)
        outgoing[h] = mm(place[...], total).astype(BF).reshape(outgoing.shape[1:])

        if h == 0:
            x_copy(2).wait_recv()
            y_copy(2).start()
        for target, owner, number in peers:
            pltpu.make_async_remote_copy(
                outgoing.at[h, pl.ds(number * 2, 2)], rows_in.at[:, my_slots, column(h)],
                row_send.at[h], row_recv.at[h], device_id=target, device_id_type=MESH,
            ).start()
        own_copy(h).start()

    for load in load_basis + load_far:
        load.wait()
    for b in range(BANDS):
        half_out[0, b * band:(b + 1) * band] = (
            mm(emb[0, far_band(b), :], own_basis[0]) + mm(emb[1, far_band(b), :], own_basis[1])
        )
        half_copy(0, b).start()
    for load in load_own:
        load.wait()
    own = mm(emb[0, own_rows, :], own_basis[0]) + mm(emb[1, own_rows, :], own_basis[1])
    for c in range(2):
        x_copy(c).wait_recv()
        y_copy(c).start()
    send_half(0, own)
    for c in range(3, CHUNKS):
        x_copy(c).wait_recv()
        y_copy(c).start()

    half_out[1] = mm(emb[0, far_rows, :], far_basis[0])
    kept[...] = mm(emb[0, own_rows, :], far_basis[0])
    for c in range(CHUNKS):
        y_copy(c).wait_recv()
    for b in range(BANDS):
        half_out[1, b * band:(b + 1) * band] += mm(emb[1, far_band(b), :], far_basis[1])
        half_copy(1, b).start()
    own = kept[...] + mm(emb[1, own_rows, :], far_basis[1])
    send_half(1, own)

    for_meta = []

    all_small(meta_recv).wait()
    for k in range(2):
        blocks = []
        for b in range(devices // chip):
            block = meta_in[b * chip, k:k + 1, :]
            for q in range(1, chip):
                block = block + meta_in[b * chip + q, k:k + 1, :]
            blocks.append(block)
        stamps = jnp.concatenate(blocks, axis=1)
        stamps = jnp.where(stamps == 0.0, float(SENTINEL), stamps)
        for_meta.append((stamps, row_to_column(stamps)))

    all_rows(row_recv.at[0]).wait()
    all_rows(row_recv.at[1]).wait()
    own_copy(0).wait()
    own_copy(1).wait()

    eye = lax.broadcasted_iota(jnp.int32, (128, 128), 0) == (
        lax.broadcasted_iota(jnp.int32, (128, 128), 1)
    )
    ret_out[...] = jnp.zeros_like(ret_out)
    inverses = []
    for k in range(2):
        keys = rows_in[k]
        scores = nt(keys, keys)
        blocks = [
            jnp.sum(
                jnp.where(eye, scores[b * 128:(b + 1) * 128, b * 128:(b + 1) * 128], 0.0),
                axis=0, keepdims=True,
            )
            for b in range(scores.shape[0] // 128)
        ]
        inverse = lax.rsqrt(jnp.concatenate(blocks, axis=1) + EPS)
        inverses.append(inverse)
        stamps, stamp_column = for_meta[k]
        scaled = scores * row_to_column(inverse)
        best = jnp.max(jnp.where(stamp_column < stamps, scaled, -jnp.inf), axis=0, keepdims=True)
        best = jnp.maximum(best * inverse, -1.0)
        for b in range(devices // chip):
            ret_out[b, k:k + 1, :] = best[:, b * 128:(b + 1) * 128]

    for target, owner, number in peers:
        pltpu.make_async_remote_copy(
            ret_out.at[owner, pl.ds(0, 2)], ret_in.at[me, pl.ds(0, 2)],
            ret_send, ret_recv, device_id=target, device_id_type=MESH,
        ).start()
    ret_in[me] = ret_out[o]

    wide = rows_in.shape[2]
    cents = []
    for k in range(2):
        high = inverses[k].astype(BF)
        low = (inverses[k] - high.astype(F32)).astype(BF)
        keys = rows_in[k]
        fill = (8, inverses[k].shape[1])
        sums = (
            mm(jnp.broadcast_to(high, fill), keys) + mm(jnp.broadcast_to(low, fill), keys)
        )[:1]
        mean = jnp.sum(sums * sums, axis=1, keepdims=True) / wide
        cents.append(sums * lax.rsqrt(mean + EPS))
    cent_out[...] = jnp.zeros_like(cent_out)
    for k in range(2):
        left, right = cents[k][:, :128], cents[k][:, 128:]
        cent_out[k:k + 1, :] = jnp.where(s == 0, right, left)
    cent_copy = pltpu.make_async_remote_copy(
        cent_out, cent_in, cent_sem.at[0], cent_sem.at[1],
        device_id=sub_peer, device_id_type=MESH,
    )
    cent_copy.start()
    all_small(ret_recv).wait()
    answers = ret_in[...].reshape(128, 128).T
    picked = jnp.zeros((128, row_count), F32)
    for _ in range(3):
        part = answers.astype(BF)
        picked = picked + mm(part, member_bf)
        answers = answers - part.astype(F32)
    sim_ref[...] = jnp.sum(jnp.where(at_lane, picked, 0.0), axis=0, keepdims=True)

    cent_copy.wait_recv()
    mine = jnp.concatenate(
        [jnp.where(s == 0, cents[k][:, :128], cents[k][:, 128:]) for k in range(2)], axis=0
    )
    theirs = cent_in[0:2, :]
    cent_ref[...] = jnp.where(
        s == 0,
        jnp.concatenate([mine, theirs], axis=0),
        jnp.concatenate([theirs, mine], axis=0),
    )

    all_small(meta_send).wait()
    all_small(ret_send).wait()
    for h in range(2):
        all_rows(row_send.at[h]).wait()
    for c in range(CHUNKS):
        x_copy(c).wait_send()
        y_copy(c).wait_send()
    for h in range(2):
        for b in range(BANDS):
            half_copy(h, b).wait_send()
    cent_copy.wait_send()


def fused(embeddings, pca_basis, assignment, row_stamp):
    row_count = assignment.shape[0]
    owners_n = lax.axis_size("owners")
    inner_n = lax.axis_size("inner")
    sub_n = lax.axis_size("sub")
    devices = owners_n * inner_n * sub_n
    clusters = KDEV * owners_n
    slots = 2 * row_count // clusters
    depth, part = pca_basis.shape
    wide = part * inner_n
    dma = pltpu.SemaphoreType.DMA
    hbm = pl.BlockSpec(memory_space=pltpu.HBM)
    vmem = pl.BlockSpec(memory_space=pltpu.VMEM)
    similarity, centroid = pl.pallas_call(
        functools.partial(fused_kernel, (inner_n, sub_n, devices, slots)),
        out_shape=(
            jax.ShapeDtypeStruct((1, row_count), F32),
            jax.ShapeDtypeStruct((KDEV // inner_n, wide // sub_n), F32),
        ),
        in_specs=[hbm, hbm, hbm, hbm],
        out_specs=(vmem, vmem),
        scratch_shapes=[
            pltpu.VMEM((2, embeddings.shape[0], depth // 2), BF),
            pltpu.VMEM((2, depth // 2, part), BF),
            pltpu.VMEM((2, depth // 2, part), BF),
            pltpu.VMEM((clusters * slots, row_count), BF),
            pltpu.VMEM((2, row_count, part), F32),
            pltpu.VMEM((2, row_count, part), F32),
            pltpu.VMEM((2, clusters, slots, part), BF),
            pltpu.VMEM((2, devices * slots, wide), BF),
            pltpu.VMEM((devices, 8, 128), F32),
            pltpu.VMEM((devices, 8, 128), F32),
            pltpu.VMEM((owners_n, 8, 128), F32),
            pltpu.VMEM((devices, 8, 128), F32),
            pltpu.VMEM((8, 128), F32),
            pltpu.VMEM((8, 128), F32),
            dma((4,)), dma((2,)), dma((CHUNKS,)), dma((CHUNKS,)), dma((CHUNKS,)), dma((CHUNKS,)),
            dma((2, BANDS)), dma((2, BANDS)),
            dma, dma, dma((2,)), dma((2,)), dma, dma,
            dma((2,)), dma((4,)),
            pltpu.VMEM((1, row_count), jnp.int32),
            pltpu.VMEM((1, row_count), jnp.int32),
            pltpu.VMEM((row_count, part), F32),
        ],
        compiler_params=pltpu.CompilerParams(
            collective_id=0, has_side_effects=True, vmem_limit_bytes=60 * 1024 * 1024
        ),
        cost_estimate=pl.CostEstimate(
            flops=2 * embeddings.size * wide, bytes_accessed=2 * embeddings.size, transcendentals=0
        ),
    )(embeddings, pca_basis, assignment.reshape(1, row_count), row_stamp.reshape(1, row_count))
    return similarity.reshape(row_count), centroid


def fits(mesh):
    size = mesh.shape
    return (size["groups"], size["inner"], size["sub"], size["owners"]) == (2, 2, 2, 4)


def solution(mesh):
    in_specs = (
        P(("groups", "owners", "inner"), "sub"),
        P("sub", "inner"),
        P(("groups", "owners", "inner", "sub"), None),
        P(("groups", "owners", "inner", "sub")),
    )
    out_specs = (P(("groups", "owners", "inner", "sub")), P(("groups", "owners", "inner"), "sub"))
    return jax.shard_map(
        fused if fits(mesh) else per_device, mesh=mesh, in_specs=in_specs, out_specs=out_specs, check_vma=False
    )
```
